32 devices in a mesh: expert: 16 (over z, y, x), shard: 2 (over core).
Axes of the slice: x: 2, y: 2, z: 4, core: 2. Of those that a mesh axis runs over, the one named last changes fastest.
Arguments:
- tokens: bfloat16 [8192, 768], P(('expert', 'shard')), may hold values from -6 to 6
- out_grad: bfloat16 [8192, 768], P(('expert', 'shard')), may hold values from -6 to 6
- seq_lengths: int32 [16, 4], P('expert'), may hold values from 1 to 384, 512 in all within a row
- expert_ids: int32 [8192, 1], P(('expert', 'shard')), may hold values from 0 to 15; in each aligned block of 256 rows (0 to 255, 256 to 511, ...) at most 32 rows name the same one
- w_query: bfloat16 [768, 768], P('shard'), may hold values from -0.21875 to 0.21875
- w_key: bfloat16 [768, 768], P('shard'), may hold values from -0.21875 to 0.21875
- w_value: bfloat16 [768, 768], P('shard'), may hold values from -0.21875 to 0.21875
- w_output: bfloat16 [768, 768], P('shard'), may hold values from -3 to 3
- w_router: bfloat16 [768, 16], P('shard'), may hold values from -0.15625 to 0.15625
- gain_attn: bfloat16 [768], P('shard'), may hold values from 0.5 to 1.5
- gain_ffn: bfloat16 [768], P('shard'), may hold values from 0.5 to 1.5
- bias_table: bfloat16 [32, 12], P('shard'), may hold values from -5 to 5
- expert_in: bfloat16 [16, 768, 3072], P('expert', None, 'shard'), may hold values from -0.21875 to 0.21875
- expert_out: bfloat16 [16, 3072, 768], P('expert', 'shard'), may hold values from -6 to 6
Outputs:
- layer_out: bfloat16 [8192, 768], P(('expert', 'shard'))
- grad_tokens: float32 [8192, 768], P(('expert', 'shard'))
- grad_w_query: float32 [768, 768], P('shard')
- grad_w_key: float32 [768, 768], P('shard')
- grad_w_value: float32 [768, 768], P('shard')
- grad_w_output: float32 [768, 768], P('shard')
- grad_w_router: float32 [768, 16], P('shard')
- grad_gain_attn: float32 [768], P('shard')
- grad_gain_ffn: float32 [768], P('shard')
- grad_bias_table: float32 [32, 12], P('shard')
- grad_expert_in: float32 [16, 768, 3072], P('expert', None, 'shard')
- grad_expert_out: float32 [16, 3072, 768], P('expert', 'shard')
The draws below stay inside these ranges and needn't reach their ends.
Inputs may be any that keep to these rules, and one draw needn't show every extreme that they name: `seq_lengths`: row c lays its sequences end to end over the 512 tokens of group c; each row sums to 512 and its largest entry is exactly 384. `expert_ids`: among the 256 tokens of one device no expert is named more than 32 times, a bound that some block reaches.
All inputs are finite; a program needn't handle non-finite values.
Results may differ from the reference program's by a relative error of at most 0.014.
The reference program's roundings to bfloat16 on the way count: a program that leaves them out, or rounds other values in their place, can miss the bound.
Values may be sent and summed in bfloat16 or wider, within the bound.
A program may use at most 128 MiB of HBM per device.

```python
import math
import jax
import jax.numpy as jnp
import numpy as np
from jax import lax

D = 768
HEADS = 12
HEAD_DIM = 64
FF = 3072
BUCKETS = 32
TOK_DEV = 256
SEQ_CHIP = 4
EXPERTS = 16
CHIPS = 16
TOKENS = 8192
LONGEST = 384
CAP = 32
N_EXPERT = 16
N_SHARD = 2


def block_levels(stream_key, extent, shards, least, top_value):
    def one(dim, shards_of):
        heights = jax.random.uniform(jax.random.fold_in(jax.random.fold_in(stream_key, 6), dim), (shards_of,), jnp.float32, least / len(shards), top_value / len(shards))
        return jnp.repeat(jnp.exp(heights), extent[dim] // shards_of).reshape((-1,) + (1,) * (len(extent) - dim - 1))

    loudness = one(*shards[0])
    for cut in shards[1:]:
        loudness = loudness * one(*cut)
    return loudness


def length_profile(number_of, total, limit, lean):
    weights = [(1 << 20) // math.isqrt(standing ** lean) + 1 for standing in range(2, number_of + 1)]
    rest, counts = total - limit - (number_of - 1), [1] * (number_of - 1)
    while rest > 0:
        movable = [i for i in range(number_of - 1) if counts[i] < limit]
        whole, remaining = sum([weights[i] for i in movable]), rest
        for i in movable:
            addition = min(limit - counts[i], max(1, remaining * weights[i] // whole), rest)
            counts[i] = counts[i] + addition
            rest = rest - addition
    return np.array([limit] + counts)


def uneven(own_key, number_of, total, most, skew):
    if number_of == 2:
        one = jax.random.randint(own_key, (), max(1, total - most), min(most, total - 1) + 1)
        return jnp.stack([one, total - one])
    sizes = jnp.asarray(length_profile(number_of, total, most, skew), jnp.int32)
    couples = (number_of - 1) // 2
    donor, sink = sizes[1:1 + 2 * couples:2], sizes[2:2 + 2 * couples:2]
    room = jnp.minimum(donor - 1, most - sink)
    shifted = jax.random.randint(jax.random.fold_in(own_key, 1), (couples,), 0, 1 << 20) % (room + 1)
    sizes = sizes.at[1:1 + 2 * couples:2].set(donor - shifted).at[2:2 + 2 * couples:2].set(sink + shifted)
    return sizes[jax.random.permutation(jax.random.fold_in(own_key, 2), number_of)]


def shared_out(own_key, own, number, rows, number_of, top, bound, slope):
    ranking = jax.random.permutation(own_key, number_of)
    heavy_load, usual = load_shares(number_of, rows * top, bound, slope, True), load_shares(number_of, rows * top, bound, slope, False)
    places = jnp.arange(number_of)

    def named(lengths, offset_by):
        used = int((lengths > 0).sum())
        fixed = max(1, used // 4)
        moved = fixed + (places - fixed + offset_by * (used - fixed)) % max(1, number_of - fixed)
        return jnp.zeros((number_of,), jnp.int32).at[ranking[jnp.where(places < fixed, places, moved)]].set(jnp.asarray(lengths, jnp.int32))

    lengths = jnp.where(number % 4 == 0, named(heavy_load, number // 4), named(usual, number - number // 4 - 1))
    mixed = jax.random.permutation(jax.random.fold_in(own, 3), number_of)
    giver, sink = mixed[0:number_of // 2 * 2:2], mixed[1:number_of // 2 * 2:2]
    room = jnp.minimum(lengths[giver] - 1, bound - lengths[sink]) // 2
    room = jnp.where((giver == ranking[0]) | (sink == ranking[0]) | (lengths[sink] == 0), 0, jnp.maximum(room, 0))
    moved = jax.random.randint(jax.random.fold_in(own, 4), (number_of // 2,), 0, 1 << 20) % (room + 1)
    lengths = lengths.at[giver].add(-moved).at[sink].add(moved)
    members = jnp.searchsorted(jnp.cumsum(lengths), jnp.arange(rows * top), side="right").astype(jnp.int32)
    listing = members.reshape(top, rows).T
    listing = listing[jax.random.permutation(jax.random.fold_in(own, 1), rows)]
    offset_by = jax.random.randint(jax.random.fold_in(own, 2), (rows, 1), 0, top)
    return jnp.take_along_axis(listing, (jnp.arange(top)[None, :] + offset_by) % top, axis=1)


def load_shares(count, total, limit, slope, full):
    loads = [(1 << 20) // math.isqrt(grade ** slope) + 1 for grade in range(1, count + 1)]
    largest = limit if full else min(limit, max(-(-total // count), total * loads[0] // sum(loads)))
    least = 1 if total - largest >= count - 1 else 0
    holding, surplus = [largest] + [least] * (count - 1), total - largest - least * (count - 1)
    while surplus > 0:
        movable = [i for i in range(1, count) if holding[i] < largest] or [i for i in range(1, count) if holding[i] < limit]
        pool, budget = sum([loads[i] for i in movable]), surplus
        for i in movable:
            addition = min(limit - holding[i], max(1, budget * loads[i] // pool), surplus)
            holding[i] = holding[i] + addition
            surplus = surplus - addition
    return np.array(holding)


def scatter_about(rng, extent, scale, limit, split=(), kind=jnp.bfloat16):
    factor_of = block_levels(rng, extent, split, -0.22, 0.18) if split else 1.0
    result = jax.random.normal(rng, extent, jnp.float32) * scale * factor_of
    return jnp.minimum(jnp.maximum(result, -limit), limit).astype(kind)


def setup_inputs(seed: int = 0) -> dict:
    key_of = jax.random.split(jax.random.key(seed), 15)
    tokens = scatter_about(key_of[0], (TOKENS, D), 1.0, 6.0, ((0, 32),))
    out_grad = scatter_about(key_of[1], (TOKENS, D), 1.0, 6.0, ((0, 32),))
    seq_lengths = jax.vmap(lambda own: uneven(own, SEQ_CHIP, 2 * TOK_DEV, LONGEST, 2))(jax.random.split(key_of[2], CHIPS)).reshape((CHIPS, SEQ_CHIP)).astype(jnp.int32)
    expert_ids_keys = jax.random.split(jax.random.fold_in(key_of[3], 1), TOKENS // TOK_DEV)
    expert_ids_turns = jax.random.permutation(jax.random.fold_in(key_of[3], 3), TOKENS // TOK_DEV)
    expert_ids = jax.vmap(lambda own, number: shared_out(jax.random.fold_in(key_of[3], 2), own, number, TOK_DEV, EXPERTS, 1, CAP, 1))(expert_ids_keys, expert_ids_turns).reshape((TOKENS, 1))
    w_query = scatter_about(key_of[4], (D, HEADS * HEAD_DIM), D ** -0.5, 0.21875, ((0, 2),))
    w_key = scatter_about(key_of[5], (D, HEADS * HEAD_DIM), D ** -0.5, 0.21875, ((0, 2),))
    w_value = scatter_about(key_of[6], (D, HEADS * HEAD_DIM), D ** -0.5, 0.21875, ((0, 2),))
    w_output = scatter_about(key_of[7], (HEADS * HEAD_DIM, D), (max(HEADS * HEAD_DIM // 192, 1)) ** -0.5, 3.0, ((0, 2),))
    w_router = scatter_about(key_of[8], (D, EXPERTS), (2 * D) ** -0.5, 0.15625, ((0, 2),))
    gain_attn = jnp.clip(1.0 + 0.1 * jax.random.normal(key_of[9], (D,), jnp.float32), 0.5, 1.5).astype(jnp.bfloat16)
    gain_ffn = jnp.clip(1.0 + 0.1 * jax.random.normal(key_of[10], (D,), jnp.float32), 0.5, 1.5).astype(jnp.bfloat16)
    bias_table = scatter_about(key_of[11], (BUCKETS, HEADS), 1.0, 5.0, ((0, 2),))
    expert_in = scatter_about(key_of[12], (EXPERTS, D, FF), D ** -0.5, 0.21875, ((0, 16), (2, 2)))
    expert_out = scatter_about(key_of[13], (EXPERTS, FF, D), (EXPERTS / 32), 6.0, ((0, 16), (1, 2)))
    return dict(tokens=tokens, out_grad=out_grad, seq_lengths=seq_lengths, expert_ids=expert_ids, w_query=w_query, w_key=w_key, w_value=w_value, w_output=w_output, w_router=w_router, gain_attn=gain_attn, gain_ffn=gain_ffn, bias_table=bias_table, expert_in=expert_in, expert_out=expert_out)


@jax.custom_vjp
def low(v):
    return lax.optimization_barrier(v.astype(jnp.bfloat16)).astype(jnp.float32)

@jax.custom_vjp
def low_back(v):
    return v

def low_keep(v):
    return (low(v), None)

def low_pass(kept, grad):
    return (grad,)

def back_keep(v):
    return (v, None)

def back_low(kept, grad):
    return (low(grad),)
low.defvjp(low_keep, low_pass)
low_back.defvjp(back_keep, back_low)
bucket_edges = (8, 12, 16, 23, 32, 46, 64, 91)
epsilon = 1e-06
score_scale = 0.125
masked_score = -1e+30
highest = lax.Precision.HIGHEST

def bucket_of(offsets):
    distance = jnp.abs(offsets)
    far_bucket = 8 + sum(((distance >= boundary).astype(jnp.int32) for boundary in bucket_edges[1:]))
    near_bucket = jnp.where(distance < 8, distance, far_bucket)
    return near_bucket + 16 * (offsets > 0).astype(jnp.int32)

def rms_scale(hidden):
    return lax.rsqrt(lax.optimization_barrier(jnp.mean(hidden * hidden, axis=-1, keepdims=True)) + epsilon)

def attend_block(query_block, key_chip, value_chip, table_heads, block_places, block_docs, chip_places, chip_docs):
    raw_scores = low_back(jnp.einsum('rhd,khd->hrk', query_block, key_chip, precision=highest) * score_scale)
    offsets = chip_places[None, :] - block_places[:, None]
    biased = raw_scores + jnp.take(table_heads, bucket_of(offsets), axis=1)
    same_doc = block_docs[:, None] == chip_docs[None, :]
    scores = jnp.where(same_doc[None], biased, masked_score)
    probabilities = jax.nn.softmax(scores, axis=-1)
    return jnp.einsum('hrk,khd->rhd', low(probabilities), value_chip, precision=highest)

def chip_attention(query_chip, key_chip, value_chip, chip_lengths, table_heads):
    group_rows = query_chip.shape[0]
    chip_places = jnp.arange(group_rows, dtype=jnp.int32)
    seq_ends = jnp.cumsum(chip_lengths)[:-1]
    chip_docs = lax.optimization_barrier(jnp.sum((chip_places[:, None] >= seq_ends[None, :]).astype(jnp.int32), axis=1))
    block_rows = min(512, TOK_DEV)
    block_count = group_rows // block_rows

    def one_block(block_inputs):
        return attend_block(block_inputs[0], key_chip, value_chip, table_heads, block_inputs[1], block_inputs[2], chip_places, chip_docs)
    outputs = lax.map(jax.checkpoint(one_block), (query_chip.reshape(block_count, block_rows, HEADS, HEAD_DIM), chip_places.reshape(block_count, block_rows), chip_docs.reshape(block_count, block_rows)))
    return outputs.reshape(query_chip.shape)

def expert_pass(expert_inputs):
    rows_in, weight_in, weight_out = expert_inputs
    pre_act = low_back(jnp.dot(rows_in, weight_in, precision=highest))
    act_low = low(jax.nn.gelu(pre_act))
    return low_back(low(jnp.dot(act_low, weight_out, precision=highest)))

def reference(tokens, out_grad, seq_lengths, expert_ids, w_query, w_key, w_value, w_output, w_router, gain_attn, gain_ffn, bias_table, expert_in, expert_out):
    devices = N_EXPERT * N_SHARD
    route_flat = expert_ids[:, 0]
    per_device = route_flat.reshape(devices, TOK_DEV)
    one_hot = (per_device[:, :, None] == jnp.arange(EXPERTS, dtype=jnp.int32)[None, None, :]).astype(jnp.int32)
    slot_ranks = lax.optimization_barrier(jnp.sum(jnp.cumsum(one_hot, axis=1) * one_hot, axis=2)) - 1
    device_rows = jnp.arange(devices, dtype=jnp.int32)[:, None]
    slot_ids = (per_device * (devices * CAP) + device_rows * CAP + slot_ranks).reshape(-1)
    route_hot = (route_flat[:, None] == jnp.arange(EXPERTS, dtype=jnp.int32)[None, :]).astype(jnp.float32)
    chip_shape = (N_EXPERT, N_SHARD * TOK_DEV, HEADS, HEAD_DIM)

    def forward(x_float, query_weight, key_weight, value_weight, output_weight, router_weight, gain_one, gain_two, bias_rows, weight_in, weight_out):
        normed_one = low(x_float * rms_scale(x_float) * gain_one)
        query_rows = low_back(low(jnp.dot(normed_one, query_weight, precision=highest)))
        key_rows = low_back(low(jnp.dot(normed_one, key_weight, precision=highest)))
        value_rows = low_back(low(jnp.dot(normed_one, value_weight, precision=highest)))
        table_heads = bias_rows.T

        def one_chip(chip_inputs):
            return chip_attention(chip_inputs[0], chip_inputs[1], chip_inputs[2], chip_inputs[3], table_heads)
        attended = lax.map(one_chip, (query_rows.reshape(chip_shape), key_rows.reshape(chip_shape), value_rows.reshape(chip_shape), seq_lengths))
        attn_low = low_back(low(attended.reshape(-1, HEADS * HEAD_DIM)))
        branch = low_back(jnp.dot(attn_low, output_weight, precision=highest))
        hidden_one = x_float + branch
        normed_two = hidden_one * rms_scale(hidden_one) * gain_two
        logits = jnp.dot(normed_two, router_weight, precision=highest)
        route_probs = jax.nn.softmax(logits, axis=-1)
        gate_value = lax.optimization_barrier(jnp.sum(route_probs * route_hot, axis=1, keepdims=True))
        expert_rows = low_back(low(normed_two))
        buffer = jnp.zeros((EXPERTS * devices * CAP, D), jnp.float32).at[slot_ids].set(expert_rows)
        results = lax.map(jax.checkpoint(expert_pass), (buffer.reshape(EXPERTS, devices * CAP, D), weight_in, weight_out))
        token_results = results.reshape(-1, D)[slot_ids]
        return hidden_one + gate_value * token_results
    layer_out, pullback = jax.vjp(forward, tokens.astype(jnp.float32), w_query.astype(jnp.float32), w_key.astype(jnp.float32), w_value.astype(jnp.float32), w_output.astype(jnp.float32), w_router.astype(jnp.float32), gain_attn.astype(jnp.float32), gain_ffn.astype(jnp.float32), bias_table.astype(jnp.float32), expert_in.astype(jnp.float32), expert_out.astype(jnp.float32))
    grads = pullback(out_grad.astype(jnp.float32))
    return (layer_out.astype(jnp.bfloat16), grads[0], grads[1], grads[2], grads[3], grads[4], grads[5], grads[6], grads[7], grads[8], grads[9], grads[10])
```

```python
import functools

import jax
import jax.numpy as jnp
from jax import lax
from jax.experimental import pallas as pl
from jax.experimental.pallas import tpu as pltpu
from jax.sharding import PartitionSpec as P

bucket_edges = (8, 12, 16, 23, 32, 46, 64, 91)
epsilon = 1e-06
score_scale = 0.125
masked_score = -1e30
highest = lax.Precision.HIGHEST
contract_last = (((1,), (1,)), ((), ()))
contract_first = (((0,), (0,)), ((), ()))


def bucket_of(offsets):
    distance = jnp.abs(offsets)
    far_bucket = 8 + sum(
        ((distance >= boundary).astype(jnp.int32) for boundary in bucket_edges[1:])
    )
    near_bucket = jnp.where(distance < 8, distance, far_bucket)
    return near_bucket + 16 * (offsets > 0).astype(jnp.int32)


def rms_forward(hidden, gain_value):
    scale = lax.rsqrt(jnp.mean(hidden * hidden, axis=-1, keepdims=True) + epsilon)
    return (hidden * scale * gain_value, scale)


def rms_backward(hidden, scale, gain_value, grad_normed):
    weighted = grad_normed * gain_value
    grad_gain = jnp.sum(grad_normed * hidden * scale, axis=0)
    grad_hidden = scale * weighted - hidden * (scale * scale * scale) * jnp.mean(
        weighted * hidden, axis=-1, keepdims=True
    )
    return (grad_hidden, grad_gain)


def toeplitz(seed_rows, row_count):
    rows = seed_rows
    while rows.shape[0] < row_count:
        rows = jnp.concatenate([rows, pltpu.roll(rows, rows.shape[0], 1)], axis=0)
    return rows


def fold_rows(block, width):
    row_count, columns = block.shape
    rows = jnp.concatenate([block, jnp.zeros((row_count, width - columns), block.dtype)], axis=1)
    while rows.shape[0] > 8:
        half = rows.shape[0] // 2
        rows = rows[:half] + pltpu.roll(rows[half:], width - half, 1)
    return rows


def attend_kernel(head_size, q_ref, k_ref, v_ref, seed_ref, qdoc_ref, kdoc_ref, o_ref, p_ref):
    row_count, key_count = q_ref.shape[0], k_ref.shape[0]
    same_doc = qdoc_ref[...] == kdoc_ref[...]
    outs = []
    for h in range(seed_ref.shape[0]):
        cols = slice(h * head_size, (h + 1) * head_size)
        bias = toeplitz(seed_ref[h], row_count)[:, :key_count]
        scores = (
            lax.dot_general(
                q_ref[:, cols], k_ref[:, cols], contract_last, preferred_element_type=jnp.float32
            )
            * score_scale
            + bias
        )
        scores = jnp.where(same_doc, scores, masked_score)
        weights = jnp.exp(scores - jnp.max(scores, axis=-1, keepdims=True))
        probs = weights / jnp.sum(weights, axis=-1, keepdims=True)
        p_ref[h] = probs
        outs.append(
            jnp.dot(probs.astype(jnp.bfloat16), v_ref[:, cols], preferred_element_type=jnp.float32)
        )
    o_ref[...] = jnp.concatenate(outs, axis=1).astype(o_ref.dtype)


def attend_back_kernel(
    head_size, width, q_ref, k_ref, v_ref, p_ref, do_ref, dq_ref, dk_ref, dv_ref, fold_ref
):
    dqs, dks, dvs = [], [], []
    for h in range(p_ref.shape[0]):
        cols = slice(h * head_size, (h + 1) * head_size)
        probs, grad_out = p_ref[h], do_ref[:, cols]
        grad_probs = lax.dot_general(
            grad_out, v_ref[:, cols], contract_last, preferred_element_type=jnp.float32
        )
        row_dot = jnp.sum(probs * grad_probs, axis=-1, keepdims=True)
        grad_scores = probs * (grad_probs - row_dot)
        fold_ref[h] = fold_rows(grad_scores, width)
        grad_low = grad_scores.astype(jnp.bfloat16)
        dqs.append(
            jnp.dot(grad_low, k_ref[:, cols], preferred_element_type=jnp.float32) * score_scale
        )
        dks.append(
            lax.dot_general(
                grad_low, q_ref[:, cols], contract_first, preferred_element_type=jnp.float32
            )
            * score_scale
        )
        dvs.append(
            lax.dot_general(
                probs.astype(jnp.bfloat16),
                grad_out,
                contract_first,
                preferred_element_type=jnp.float32,
            )
        )
    dq_ref[...] = jnp.concatenate(dqs, axis=1).astype(dq_ref.dtype)
    dk_ref[...] = jnp.concatenate(dks, axis=1).astype(dk_ref.dtype)
    dv_ref[...] = jnp.concatenate(dvs, axis=1).astype(dv_ref.dtype)


def attend_forward(queries, keys_values, seed_rows, query_docs, key_docs, head_size):
    rows, width = queries.shape
    keys = keys_values.shape[0]
    heads, _, lanes = seed_rows.shape
    pair = 128 // head_size
    steps = heads // pair
    return pl.pallas_call(
        functools.partial(attend_kernel, head_size),
        grid=(steps,),
        in_specs=[
            pl.BlockSpec((rows, 128), lambda i: (0, i)),
            pl.BlockSpec((keys, 128), lambda i: (0, i)),
            pl.BlockSpec((keys, 128), lambda i: (0, i + steps)),
            pl.BlockSpec((pair, 8, lanes), lambda i: (i, 0, 0)),
            pl.BlockSpec((rows, 1), lambda i: (0, 0)),
            pl.BlockSpec((1, keys), lambda i: (0, 0)),
        ],
        out_specs=[
            pl.BlockSpec((rows, 128), lambda i: (0, i)),
            pl.BlockSpec((pair, rows, keys), lambda i: (i, 0, 0)),
        ],
        out_shape=[
            jax.ShapeDtypeStruct((rows, width), jnp.bfloat16),
            jax.ShapeDtypeStruct((heads, rows, keys), jnp.float32),
        ],
        compiler_params=pltpu.CompilerParams(vmem_limit_bytes=40 << 20),
        cost_estimate=pl.CostEstimate(
            flops=4 * rows * keys * width, bytes_accessed=8 << 20, transcendentals=0
        ),
        name="attend_forward",
    )(queries, keys_values, keys_values, seed_rows, query_docs[:, None], key_docs[None, :])


def attend_backward(queries, keys_values, probs, grad_attn, head_size, lanes):
    rows, width = queries.shape
    keys = keys_values.shape[0]
    heads = probs.shape[0]
    pair = 128 // head_size
    steps = heads // pair
    row_spec = pl.BlockSpec((rows, 128), lambda i: (0, i))
    key_spec = pl.BlockSpec((keys, 128), lambda i: (0, i))
    return pl.pallas_call(
        functools.partial(attend_back_kernel, head_size, lanes),
        grid=(steps,),
        in_specs=[
            row_spec,
            key_spec,
            pl.BlockSpec((keys, 128), lambda i: (0, i + steps)),
            pl.BlockSpec((pair, rows, keys), lambda i: (i, 0, 0)),
            row_spec,
        ],
        out_specs=[
            row_spec,
            key_spec,
            key_spec,
            pl.BlockSpec((pair, 8, lanes), lambda i: (i, 0, 0)),
        ],
        out_shape=[
            jax.ShapeDtypeStruct((rows, width), jnp.bfloat16),
            jax.ShapeDtypeStruct((keys, width), jnp.bfloat16),
            jax.ShapeDtypeStruct((keys, width), jnp.bfloat16),
            jax.ShapeDtypeStruct((heads, 8, lanes), jnp.float32),
        ],
        compiler_params=pltpu.CompilerParams(vmem_limit_bytes=40 << 20),
        cost_estimate=pl.CostEstimate(
            flops=8 * rows * keys * width, bytes_accessed=9 << 20, transcendentals=0
        ),
        name="attend_backward",
    )(queries, keys_values, keys_values, probs, grad_attn)


def on_device(
    tokens,
    out_grad,
    seq_lengths,
    expert_ids,
    w_query,
    w_key,
    w_value,
    w_output,
    w_router,
    gain_attn,
    gain_ffn,
    bias_table,
    expert_in,
    expert_out,
):
    tok_count, width = tokens.shape
    half_width = w_query.shape[0]
    experts = w_router.shape[1]
    capacity = 2 * tok_count // experts
    half_buckets, heads = bias_table.shape
    buckets = 2 * half_buckets
    inner = w_query.shape[1]
    head_size = inner // heads
    shard_count = lax.axis_size("shard")
    shard_index = lax.axis_index("shard")
    key_count = shard_count * tok_count
    low, f32 = jnp.bfloat16, jnp.float32

    def dot(a, b):
        return jnp.dot(a, b, preferred_element_type=f32)

    def dot_tn(a, b):
        return lax.dot_general(a, b, contract_first, preferred_element_type=f32)

    def dot_nt(a, b):
        return lax.dot_general(a, b, contract_last, preferred_element_type=f32)

    def column(flat):
        flat = flat.reshape(-1)
        return jnp.pad(flat, (0, half_width - flat.shape[0]))[:, None]

    small = jnp.concatenate([w_router, gain_attn[:, None], gain_ffn[:, None], column(bias_table)], 1)
    small = lax.all_gather(small, "shard", axis=0, tiled=True)
    qkv_weight = lax.all_gather(
        jnp.concatenate([w_query, w_key, w_value], axis=1), "shard", axis=0, tiled=True
    )
    output_weight = lax.all_gather(w_output, "shard", axis=0, tiled=True)
    router_float = small[:, :experts].astype(f32)
    gain_one = small[:, experts].astype(f32)
    gain_two = small[:, experts + 1].astype(f32)
    table = (
        small[:, experts + 2]
        .reshape(shard_count, half_width)[:, : half_buckets * heads]
        .reshape(buckets, heads)
        .astype(f32)
    )
    x_float = tokens.astype(f32)
    normed_one, scale_one = rms_forward(x_float, gain_one)
    normed_low = normed_one.astype(low)
    kv_local = dot(normed_low, qkv_weight[:, inner:]).astype(low)
    keys_values = lax.all_gather(kv_local, "shard", axis=0, tiled=True)
    queries = dot(normed_low, qkv_weight[:, :inner]).astype(low)

    lanes = key_count + tok_count
    lane = jnp.arange(lanes, dtype=jnp.int32)
    offsets = jnp.where(lane < key_count, lane, lane - lanes) - shard_index * tok_count
    bucket_hot = (
        bucket_of(offsets)[:, None] == jnp.arange(buckets, dtype=jnp.int32)[None, :]
    ).astype(f32)
    offset_bias = jnp.einsum("lb,bh->hl", bucket_hot, table, precision=highest)
    seed_rows = jnp.stack([jnp.roll(offset_bias, r, axis=1) for r in range(8)], axis=1)

    seq_ends = jnp.cumsum(seq_lengths[0])[:-1]
    key_places = jnp.arange(key_count, dtype=jnp.int32)
    key_docs = jnp.sum((key_places[:, None] >= seq_ends[None, :]).astype(jnp.int32), axis=1)
    query_docs = lax.dynamic_slice_in_dim(key_docs, shard_index * tok_count, tok_count, 0)
    attn_part, probs = attend_forward(
        queries, keys_values, seed_rows, query_docs, key_docs, head_size
    )
    hidden_one = x_float + dot(attn_part, output_weight)
    normed_two, scale_two = rms_forward(hidden_one, gain_two)
    logits = jnp.dot(normed_two, router_float, precision=highest)
    route_probs = jax.nn.softmax(logits, axis=-1)
    route_flat = expert_ids[:, 0]
    expert_range = jnp.arange(experts, dtype=jnp.int32)
    route_int = (route_flat[:, None] == expert_range[None, :]).astype(jnp.int32)
    route_hot = route_int.astype(f32)
    gate_value = jnp.sum(route_probs * route_hot, axis=1)
    tok_range = jnp.arange(tok_count, dtype=jnp.int32)
    earlier = (tok_range[:, None] >= tok_range[None, :]).astype(low)
    counts = dot(earlier, route_hot.astype(low))
    slot_ranks = jnp.sum(counts * route_hot, axis=1).astype(jnp.int32) - 1
    slot_ids = route_flat * capacity + slot_ranks
    slot_hot = (
        slot_ids[:, None] == jnp.arange(experts * capacity, dtype=jnp.int32)[None, :]
    ).astype(low)

    def dispatch(rows):
        sent = dot_tn(slot_hot, rows).astype(low).reshape(experts, capacity, width)
        got = lax.all_to_all(sent, "expert", split_axis=0, concat_axis=0, tiled=True)
        return lax.all_gather(got, "shard", axis=0, tiled=True).reshape(-1, width)

    def collect(rows):
        halves = lax.psum_scatter(
            rows.reshape(shard_count * experts, capacity, width).astype(low),
            "shard",
            scatter_dimension=0,
            tiled=True,
        )
        got = lax.all_to_all(halves, "expert", split_axis=0, concat_axis=0, tiled=True)
        return dot(slot_hot, got.reshape(-1, width))

    grad_out = out_grad.astype(f32)
    expert_rows = dispatch(normed_two.astype(low))
    grad_rows = dispatch((gate_value[:, None] * grad_out).astype(low))
    weight_in = expert_in[0]
    weight_out = expert_out[0]
    pre_act = dot(expert_rows, weight_in)
    act_low = jax.nn.gelu(pre_act).astype(low)
    result_float = collect(dot(act_low, weight_out))
    grad_act = dot_nt(grad_rows, weight_out)
    _, gelu_pull = jax.vjp(jax.nn.gelu, pre_act)
    grad_pre = gelu_pull(grad_act)[0].astype(low)
    grad_expert_tok = collect(dot_nt(grad_pre, weight_in))

    layer_out = (hidden_one + gate_value[:, None] * result_float).astype(low)
    grad_gate = jnp.sum(grad_out * result_float, axis=1)
    grad_logits = gate_value[:, None] * (route_hot - route_probs) * grad_gate[:, None]
    grad_router = jnp.einsum("td,te->de", normed_two, grad_logits, precision=highest)
    grad_normed_two = (
        jnp.einsum("te,de->td", grad_logits, router_float, precision=highest) + grad_expert_tok
    )
    grad_hidden_norm, grad_gain_two = rms_backward(hidden_one, scale_two, gain_two, grad_normed_two)
    grad_hidden = grad_out + grad_hidden_norm
    grad_branch = grad_hidden.astype(low)

    def whole_sum(parts):
        packed = jnp.concatenate([part.astype(low) for part in parts], axis=1)
        extra = -packed.shape[1] % 128
        packed = jnp.pad(packed, ((0, 0), (0, extra)))
        halves = lax.psum_scatter(packed, "shard", scatter_dimension=0, tiled=True)
        return lax.psum(halves, "expert").astype(f32)

    first_sum = whole_sum([dot_tn(attn_part, grad_branch), grad_router, grad_gain_two[:, None]])
    grad_attn = dot_nt(grad_branch, output_weight).astype(low)
    grad_queries, grad_k_part, grad_v_part, folded = attend_backward(
        queries, keys_values, probs, grad_attn, head_size, lanes
    )
    grad_kv = lax.psum_scatter(
        jnp.concatenate([grad_k_part, grad_v_part], axis=1),
        "shard",
        scatter_dimension=0,
        tiled=True,
    )
    offset_sums = sum(jnp.roll(folded[:, r], -r, axis=1) for r in range(8))
    grad_table = jnp.einsum("hl,lb->bh", offset_sums, bucket_hot, precision=highest)
    table_column = jnp.pad(
        grad_table.reshape(shard_count, half_buckets * heads),
        ((0, 0), (0, half_width - half_buckets * heads)),
    ).reshape(-1, 1)
    grad_qkv = jnp.concatenate([grad_queries, grad_kv], axis=1)
    grad_normed_one = dot_nt(grad_qkv, qkv_weight)
    grad_x_norm, grad_gain_one = rms_backward(x_float, scale_one, gain_one, grad_normed_one)
    grad_tokens = grad_hidden + grad_x_norm
    second_sum = whole_sum([dot_tn(normed_low, grad_qkv), grad_gain_one[:, None], table_column])
    grad_w_out = dot_tn(act_low, grad_rows)
    grad_w_in = dot_tn(expert_rows, grad_pre)
    return (
        layer_out,
        grad_tokens,
        second_sum[:, :inner],
        second_sum[:, inner : 2 * inner],
        second_sum[:, 2 * inner : 3 * inner],
        first_sum[:, :width],
        first_sum[:, width : width + experts],
        second_sum[:, 3 * inner],
        first_sum[:, width + experts],
        second_sum[: half_buckets * heads, 3 * inner + 1].reshape(half_buckets, heads),
        grad_w_in[None],
        grad_w_out[None],
    )


def solution(mesh):
    placed = (
        P(("expert", "shard"), None),
        P(("expert", "shard"), None),
        P("expert", None),
        P(("expert", "shard"), None),
        P("shard", None),
        P("shard", None),
        P("shard", None),
        P("shard", None),
        P("shard", None),
        P("shard"),
        P("shard"),
        P("shard", None),
        P("expert", None, "shard"),
        P("expert", "shard", None),
    )
    return jax.shard_map(
        on_device,
        mesh=mesh,
        in_specs=placed,
        out_specs=(
            P(("expert", "shard"), None),
            P(("expert", "shard"), None),
            P("shard", None),
            P("shard", None),
            P("shard", None),
            P("shard", None),
            P("shard", None),
            P("shard"),
            P("shard"),
            P("shard", None),
            P("expert", None, "shard"),
            P("expert", "shard", None),
        ),
        check_vma=False,
    )
```

```python
import functools

import jax
import jax.numpy as jnp
from jax import lax
from jax.experimental import pallas as pl
from jax.experimental.pallas import tpu as pltpu
from jax.sharding import PartitionSpec as P

bucket_edges = (8, 12, 16, 23, 32, 46, 64, 91)
epsilon = 1e-06
score_scale = 0.125
masked_score = -1e30
highest = lax.Precision.HIGHEST
MESH = pl.DeviceIdType.MESH
contract_last = (((1,), (1,)), ((), ()))
contract_first = (((0,), (0,)), ((), ()))


def bucket_of(offsets):
    distance = jnp.abs(offsets)
    far_bucket = 8 + sum(
        ((distance >= boundary).astype(jnp.int32) for boundary in bucket_edges[1:])
    )
    near_bucket = jnp.where(distance < 8, distance, far_bucket)
    return near_bucket + 16 * (offsets > 0).astype(jnp.int32)


def rms_forward(hidden, gain_value):
    scale = lax.rsqrt(jnp.mean(hidden * hidden, axis=-1, keepdims=True) + epsilon)
    return (hidden * scale * gain_value, scale)


def rms_backward(hidden, scale, gain_value, grad_normed):
    weighted = grad_normed * gain_value
    grad_gain = jnp.sum(grad_normed * hidden * scale, axis=0)
    grad_hidden = scale * weighted - hidden * (scale * scale * scale) * jnp.mean(
        weighted * hidden, axis=-1, keepdims=True
    )
    return (grad_hidden, grad_gain)


def toeplitz(seed_rows, row_count):
    rows = seed_rows
    while rows.shape[0] < row_count:
        rows = jnp.concatenate([rows, pltpu.roll(rows, rows.shape[0], 1)], axis=0)
    return rows


def fold_rows(block, width):
    row_count, columns = block.shape
    rows = jnp.concatenate([block, jnp.zeros((row_count, width - columns), block.dtype)], axis=1)
    while rows.shape[0] > 8:
        half = rows.shape[0] // 2
        rows = rows[:half] + pltpu.roll(rows[half:], width - half, 1)
    return rows


def attend_kernel(head_size, q_ref, k_ref, v_ref, seed_ref, qdoc_ref, kdoc_ref, o_ref, p_ref):
    row_count, key_count = q_ref.shape[0], k_ref.shape[0]
    same_doc = qdoc_ref[...] == kdoc_ref[...]
    outs = []
    for h in range(seed_ref.shape[0]):
        cols = slice(h * head_size, (h + 1) * head_size)
        bias = toeplitz(seed_ref[h], row_count)[:, :key_count]
        scores = (
            lax.dot_general(
                q_ref[:, cols], k_ref[:, cols], contract_last, preferred_element_type=jnp.float32
            )
            * score_scale
            + bias
        )
        scores = jnp.where(same_doc, scores, masked_score)
        weights = jnp.exp(scores - jnp.max(scores, axis=-1, keepdims=True))
        probs = weights / jnp.sum(weights, axis=-1, keepdims=True)
        p_ref[h] = probs
        outs.append(
            jnp.dot(probs.astype(jnp.bfloat16), v_ref[:, cols], preferred_element_type=jnp.float32)
        )
    o_ref[...] = jnp.concatenate(outs, axis=1).astype(o_ref.dtype)


def attend_back_kernel(
    head_size, width, q_ref, k_ref, v_ref, p_ref, do_ref, dq_ref, dk_ref, dv_ref, fold_ref
):
    dqs, dks, dvs = [], [], []
    for h in range(p_ref.shape[0]):
        cols = slice(h * head_size, (h + 1) * head_size)
        probs, grad_out = p_ref[h], do_ref[:, cols]
        grad_probs = lax.dot_general(
            grad_out, v_ref[:, cols], contract_last, preferred_element_type=jnp.float32
        )
        row_dot = jnp.sum(probs * grad_probs, axis=-1, keepdims=True)
        grad_scores = probs * (grad_probs - row_dot)
        fold_ref[h] = fold_rows(grad_scores, width)
        grad_low = grad_scores.astype(jnp.bfloat16)
        dqs.append(
            jnp.dot(grad_low, k_ref[:, cols], preferred_element_type=jnp.float32) * score_scale
        )
        dks.append(
            lax.dot_general(
                grad_low, q_ref[:, cols], contract_first, preferred_element_type=jnp.float32
            )
            * score_scale
        )
        dvs.append(
            lax.dot_general(
                probs.astype(jnp.bfloat16),
                grad_out,
                contract_first,
                preferred_element_type=jnp.float32,
            )
        )
    dq_ref[...] = jnp.concatenate(dqs, axis=1).astype(dq_ref.dtype)
    dk_ref[...] = jnp.concatenate(dks, axis=1).astype(dk_ref.dtype)
    dv_ref[...] = jnp.concatenate(dvs, axis=1).astype(dv_ref.dtype)


def attend_forward(queries, keys_values, seed_rows, query_docs, key_docs, head_size):
    rows, width = queries.shape
    keys = keys_values.shape[0]
    heads, _, lanes = seed_rows.shape
    pair = 128 // head_size
    steps = heads // pair
    return pl.pallas_call(
        functools.partial(attend_kernel, head_size),
        grid=(steps,),
        in_specs=[
            pl.BlockSpec((rows, 128), lambda i: (0, i)),
            pl.BlockSpec((keys, 128), lambda i: (0, i)),
            pl.BlockSpec((keys, 128), lambda i: (0, i + steps)),
            pl.BlockSpec((pair, 8, lanes), lambda i: (i, 0, 0)),
            pl.BlockSpec((rows, 1), lambda i: (0, 0)),
            pl.BlockSpec((1, keys), lambda i: (0, 0)),
        ],
        out_specs=[
            pl.BlockSpec((rows, 128), lambda i: (0, i)),
            pl.BlockSpec((pair, rows, keys), lambda i: (i, 0, 0)),
        ],
        out_shape=[
            jax.ShapeDtypeStruct((rows, width), jnp.bfloat16),
            jax.ShapeDtypeStruct((heads, rows, keys), jnp.float32),
        ],
        compiler_params=pltpu.CompilerParams(vmem_limit_bytes=40 << 20),
        cost_estimate=pl.CostEstimate(
            flops=4 * rows * keys * width, bytes_accessed=8 << 20, transcendentals=0
        ),
        name="attend_forward",
    )(queries, keys_values, keys_values, seed_rows, query_docs[:, None], key_docs[None, :])


def attend_backward(queries, keys_values, probs, grad_attn, head_size, lanes):
    rows, width = queries.shape
    keys = keys_values.shape[0]
    heads = probs.shape[0]
    pair = 128 // head_size
    steps = heads // pair
    row_spec = pl.BlockSpec((rows, 128), lambda i: (0, i))
    key_spec = pl.BlockSpec((keys, 128), lambda i: (0, i))
    return pl.pallas_call(
        functools.partial(attend_back_kernel, head_size, lanes),
        grid=(steps,),
        in_specs=[
            row_spec,
            key_spec,
            pl.BlockSpec((keys, 128), lambda i: (0, i + steps)),
            pl.BlockSpec((pair, rows, keys), lambda i: (i, 0, 0)),
            row_spec,
        ],
        out_specs=[
            row_spec,
            key_spec,
            key_spec,
            pl.BlockSpec((pair, 8, lanes), lambda i: (i, 0, 0)),
        ],
        out_shape=[
            jax.ShapeDtypeStruct((rows, width), jnp.bfloat16),
            jax.ShapeDtypeStruct((keys, width), jnp.bfloat16),
            jax.ShapeDtypeStruct((keys, width), jnp.bfloat16),
            jax.ShapeDtypeStruct((heads, 8, lanes), jnp.float32),
        ],
        compiler_params=pltpu.CompilerParams(vmem_limit_bytes=40 << 20),
        cost_estimate=pl.CostEstimate(
            flops=8 * rows * keys * width, bytes_accessed=9 << 20, transcendentals=0
        ),
        name="attend_backward",
    )(queries, keys_values, keys_values, probs, grad_attn)


def stream_orders(bits):
    if bits == 4:
        return ((0, 1, 2, 3), (1, 2, 0, 3), (2, 0, 1, 3))
    return tuple(tuple((t + s) % bits for t in range(bits)) for s in range(3))


def sum_kernel(orders, cuts, x_ref, out_ref, acc, twin, held, whole, send_sem, recv_sem):
    expert, shard = lax.axis_index("expert"), lax.axis_index("shard")
    units = acc.shape[0]
    bits = len(orders[0])
    my_bits = [lax.rem(expert // (1 << b), 2) for b in range(bits)]
    partners = [expert + (1 << b) * (1 - 2 * my_bits[b]) for b in range(bits)]

    barrier = pltpu.get_barrier_semaphore()
    pl.semaphore_signal(barrier, inc=1, device_id=(expert, 1 - shard), device_id_type=MESH)
    for b in range(bits):
        pl.semaphore_signal(barrier, inc=1, device_id=(partners[b], shard), device_id_type=MESH)
    pl.semaphore_wait(barrier, bits + 1)

    def copy(source, target, stream, step, device):
        return pltpu.make_async_remote_copy(
            src_ref=source,
            dst_ref=target,
            send_sem=send_sem.at[stream, step],
            recv_sem=recv_sem.at[stream, step],
            device_id=device,
            device_id_type=MESH,
        )

    spans, keeps = [], []
    for order in orders:
        low_end, size, sends, kept = 0, units, [], []
        for b in order:
            size //= 2
            sends.append(low_end + (1 - my_bits[b]) * size)
            low_end = low_end + my_bits[b] * size
            kept.append(low_end)
        spans.append(sends)
        keeps.append(kept)

    def halves(stream, step):
        size = units >> (step + 1)
        first = units - 2 * size
        return size, first

    def begin(stream, step):
        cols = pl.ds(cuts[stream], cuts[stream + 1] - cuts[stream])
        if step < 0:
            moved = copy(
                x_ref.at[1 - shard, :, :, cols],
                twin.at[:, :, cols],
                stream,
                0,
                (expert, 1 - shard),
            )
        elif step < bits:
            size, first = halves(stream, step)
            moved = copy(
                acc.at[pl.ds(spans[stream][step], size), :, cols],
                held.at[pl.ds(first, size), :, cols],
                stream,
                1 + step,
                (partners[orders[stream][step]], shard),
            )
        else:
            back = 2 * bits - 1 - step
            size, _ = halves(stream, back)
            block = whole.at[pl.ds(keeps[stream][back], size), :, cols]
            moved = copy(block, block, stream, 1 + step, (partners[orders[stream][back]], shard))
        moved.start()
        return moved

    def add(stream, step):
        cols = slice(cuts[stream], cuts[stream + 1])
        if step < 0:

            def one(unit, carry):
                total = x_ref[shard, unit, :, cols].astype(jnp.float32) + twin[
                    unit, :, cols
                ].astype(jnp.float32)
                acc[unit, :, cols] = total.astype(acc.dtype)
                return carry

            lax.fori_loop(0, units, one, 0)
        elif step < bits:
            size, first = halves(stream, step)
            base = keeps[stream][step]
            target = whole if step == bits - 1 else acc

            def one(unit, carry):
                total = acc[base + unit, :, cols].astype(jnp.float32) + held[
                    first + unit, :, cols
                ].astype(jnp.float32)
                target[base + unit, :, cols] = total.astype(acc.dtype)
                return carry

            lax.fori_loop(0, size, one, 0)

    streams = range(len(orders))
    moving = [begin(s, -1) for s in streams]
    for step in range(-1, 2 * bits):
        for s in streams:
            moving[s].wait()
            add(s, step)
            if step + 1 < 2 * bits:
                moving[s] = begin(s, step + 1)

    def give(unit, carry):
        out_ref[unit] = whole[unit]
        return carry

    lax.fori_loop(0, units, give, 0)


def sum_over_all(packed, bits):
    shards, units, rows, columns = packed.shape
    groups = columns // 128
    cuts = [0, groups // 3 * 128, 2 * (groups // 3) * 128, columns]
    orders = stream_orders(bits)
    steps = 2 * bits + 1
    return pl.pallas_call(
        functools.partial(sum_kernel, orders, cuts),
        out_shape=jax.ShapeDtypeStruct((units, rows, columns), packed.dtype),
        in_specs=[pl.BlockSpec(memory_space=pltpu.VMEM)],
        out_specs=pl.BlockSpec(memory_space=pltpu.VMEM),
        scratch_shapes=[
            pltpu.VMEM((units, rows, columns), packed.dtype),
            pltpu.VMEM((units, rows, columns), packed.dtype),
            pltpu.VMEM((units, rows, columns), packed.dtype),
            pltpu.VMEM((units, rows, columns), packed.dtype),
            pltpu.SemaphoreType.DMA((3, steps)),
            pltpu.SemaphoreType.DMA((3, steps)),
        ],
        compiler_params=pltpu.CompilerParams(
            collective_id=0, has_side_effects=True, vmem_limit_bytes=40 << 20
        ),
        name="sum_over_all",
    )(packed)


def on_device(
    tokens,
    out_grad,
    seq_lengths,
    expert_ids,
    w_query,
    w_key,
    w_value,
    w_output,
    w_router,
    gain_attn,
    gain_ffn,
    bias_table,
    expert_in,
    expert_out,
):
    tok_count, width = tokens.shape
    half_width = w_query.shape[0]
    experts = w_router.shape[1]
    capacity = 2 * tok_count // experts
    half_buckets, heads = bias_table.shape
    buckets = 2 * half_buckets
    inner = w_query.shape[1]
    head_size = inner // heads
    shard_count = lax.axis_size("shard")
    shard_index = lax.axis_index("shard")
    key_count = shard_count * tok_count
    low, f32 = jnp.bfloat16, jnp.float32

    def dot(a, b):
        return jnp.dot(a, b, preferred_element_type=f32)

    def dot_tn(a, b):
        return lax.dot_general(a, b, contract_first, preferred_element_type=f32)

    def dot_nt(a, b):
        return lax.dot_general(a, b, contract_last, preferred_element_type=f32)

    def column(flat):
        flat = flat.reshape(-1)
        return jnp.pad(flat, (0, half_width - flat.shape[0]))[:, None]

    small = jnp.concatenate([w_router, gain_attn[:, None], gain_ffn[:, None], column(bias_table)], 1)
    small = lax.all_gather(small, "shard", axis=0, tiled=True)
    qkv_weight = lax.all_gather(
        jnp.concatenate([w_query, w_key, w_value], axis=1), "shard", axis=0, tiled=True
    )
    output_weight = lax.all_gather(w_output, "shard", axis=0, tiled=True)
    router_float = small[:, :experts].astype(f32)
    gain_one = small[:, experts].astype(f32)
    gain_two = small[:, experts + 1].astype(f32)
    table = (
        small[:, experts + 2]
        .reshape(shard_count, half_width)[:, : half_buckets * heads]
        .reshape(buckets, heads)
        .astype(f32)
    )
    x_float = tokens.astype(f32)
    normed_one, scale_one = rms_forward(x_float, gain_one)
    normed_low = normed_one.astype(low)
    kv_local = dot(normed_low, qkv_weight[:, inner:]).astype(low)
    keys_values = lax.all_gather(kv_local, "shard", axis=0, tiled=True)
    queries = dot(normed_low, qkv_weight[:, :inner]).astype(low)

    lanes = key_count + tok_count
    lane = jnp.arange(lanes, dtype=jnp.int32)
    offsets = jnp.where(lane < key_count, lane, lane - lanes) - shard_index * tok_count
    bucket_hot = (
        bucket_of(offsets)[:, None] == jnp.arange(buckets, dtype=jnp.int32)[None, :]
    ).astype(f32)
    offset_bias = jnp.einsum("lb,bh->hl", bucket_hot, table, precision=highest)
    seed_rows = jnp.stack([jnp.roll(offset_bias, r, axis=1) for r in range(8)], axis=1)

    seq_ends = jnp.cumsum(seq_lengths[0])[:-1]
    key_places = jnp.arange(key_count, dtype=jnp.int32)
    key_docs = jnp.sum((key_places[:, None] >= seq_ends[None, :]).astype(jnp.int32), axis=1)
    query_docs = lax.dynamic_slice_in_dim(key_docs, shard_index * tok_count, tok_count, 0)
    attn_part, probs = attend_forward(
        queries, keys_values, seed_rows, query_docs, key_docs, head_size
    )
    hidden_one = x_float + dot(attn_part, output_weight)
    normed_two, scale_two = rms_forward(hidden_one, gain_two)
    logits = jnp.dot(normed_two, router_float, precision=highest)
    route_probs = jax.nn.softmax(logits, axis=-1)
    route_flat = expert_ids[:, 0]
    expert_range = jnp.arange(experts, dtype=jnp.int32)
    route_int = (route_flat[:, None] == expert_range[None, :]).astype(jnp.int32)
    route_hot = route_int.astype(f32)
    gate_value = jnp.sum(route_probs * route_hot, axis=1)
    tok_range = jnp.arange(tok_count, dtype=jnp.int32)
    earlier = (tok_range[:, None] >= tok_range[None, :]).astype(low)
    counts = dot(earlier, route_hot.astype(low))
    slot_ranks = jnp.sum(counts * route_hot, axis=1).astype(jnp.int32) - 1
    slot_ids = route_flat * capacity + slot_ranks
    slot_hot = (
        slot_ids[:, None] == jnp.arange(experts * capacity, dtype=jnp.int32)[None, :]
    ).astype(low)

    def dispatch(rows):
        sent = dot_tn(slot_hot, rows).astype(low).reshape(experts, capacity, width)
        got = lax.all_to_all(sent, "expert", split_axis=0, concat_axis=0, tiled=True)
        return lax.all_gather(got, "shard", axis=0, tiled=True).reshape(-1, width)

    def collect(rows):
        halves = lax.psum_scatter(
            rows.reshape(shard_count * experts, capacity, width).astype(low),
            "shard",
            scatter_dimension=0,
            tiled=True,
        )
        got = lax.all_to_all(halves, "expert", split_axis=0, concat_axis=0, tiled=True)
        return dot(slot_hot, got.reshape(-1, width))

    grad_out = out_grad.astype(f32)
    expert_rows = dispatch(normed_two.astype(low))
    grad_rows = dispatch((gate_value[:, None] * grad_out).astype(low))
    weight_in = expert_in[0]
    weight_out = expert_out[0]
    pre_act = dot(expert_rows, weight_in)
    act_low = jax.nn.gelu(pre_act).astype(low)
    result_float = collect(dot(act_low, weight_out))
    grad_act = dot_nt(grad_rows, weight_out)
    _, gelu_pull = jax.vjp(jax.nn.gelu, pre_act)
    grad_pre = gelu_pull(grad_act)[0].astype(low)
    grad_expert_tok = collect(dot_nt(grad_pre, weight_in))

    layer_out = (hidden_one + gate_value[:, None] * result_float).astype(low)
    grad_gate = jnp.sum(grad_out * result_float, axis=1)
    grad_logits = gate_value[:, None] * (route_hot - route_probs) * grad_gate[:, None]
    grad_router = jnp.einsum("td,te->de", normed_two, grad_logits, precision=highest)
    grad_normed_two = (
        jnp.einsum("te,de->td", grad_logits, router_float, precision=highest) + grad_expert_tok
    )
    grad_hidden_norm, grad_gain_two = rms_backward(hidden_one, scale_two, gain_two, grad_normed_two)
    grad_hidden = grad_out + grad_hidden_norm
    grad_branch = grad_hidden.astype(low)

    grad_attn = dot_nt(grad_branch, output_weight).astype(low)
    grad_queries, grad_k_part, grad_v_part, folded = attend_backward(
        queries, keys_values, probs, grad_attn, head_size, lanes
    )
    grad_kv = lax.psum_scatter(
        jnp.concatenate([grad_k_part, grad_v_part], axis=1),
        "shard",
        scatter_dimension=0,
        tiled=True,
    )
    offset_sums = sum(jnp.roll(folded[:, r], -r, axis=1) for r in range(8))
    grad_table = jnp.einsum("hl,lb->bh", offset_sums, bucket_hot, precision=highest)
    table_column = jnp.pad(
        grad_table.reshape(shard_count, half_buckets * heads),
        ((0, 0), (0, half_width - half_buckets * heads)),
    ).reshape(-1, 1)
    grad_qkv = jnp.concatenate([grad_queries, grad_kv], axis=1)
    grad_normed_one = dot_nt(grad_qkv, qkv_weight)
    grad_x_norm, grad_gain_one = rms_backward(x_float, scale_one, gain_one, grad_normed_one)
    grad_tokens = grad_hidden + grad_x_norm
    narrow = [grad_router, grad_gain_two[:, None], grad_gain_one[:, None], table_column]
    parts = [dot_tn(normed_low, grad_qkv), dot_tn(attn_part, grad_branch)] + narrow
    used = sum(part.shape[1] for part in parts)
    parts.append(jnp.zeros((width, -used % 256), low))
    packed = jnp.concatenate([part.astype(low) for part in parts], axis=1)
    total_columns = packed.shape[1]
    devices = lax.axis_size("expert")
    bits = devices.bit_length() - 1
    unit_rows = shard_count * half_width // devices
    if devices == 1 << bits and unit_rows % 16 == 0:
        packed = packed.reshape(shard_count, half_width, 2, total_columns // 2)
        packed = packed.transpose(0, 2, 1, 3).reshape(shard_count, devices, unit_rows, -1)
        summed = sum_over_all(packed, bits).reshape(2, half_width, -1)
        summed = jnp.concatenate([summed[0], summed[1]], axis=1)
    else:
        halves = lax.psum_scatter(packed, "shard", scatter_dimension=0, tiled=True)
        summed = lax.psum(halves, "expert")
    summed = summed.astype(f32)
    weights_end = 3 * inner + width
    router_end = weights_end + experts
    grad_w_out = dot_tn(act_low, grad_rows)
    grad_w_in = dot_tn(expert_rows, grad_pre)
    return (
        layer_out,
        grad_tokens,
        summed[:, :inner],
        summed[:, inner : 2 * inner],
        summed[:, 2 * inner : 3 * inner],
        summed[:, 3 * inner : weights_end],
        summed[:, weights_end:router_end],
        summed[:, router_end + 1],
        summed[:, router_end],
        summed[: half_buckets * heads, router_end + 2].reshape(half_buckets, heads),
        grad_w_in[None],
        grad_w_out[None],
    )


def solution(mesh):
    placed = (
        P(("expert", "shard"), None),
        P(("expert", "shard"), None),
        P("expert", None),
        P(("expert", "shard"), None),
        P("shard", None),
        P("shard", None),
        P("shard", None),
        P("shard", None),
        P("shard", None),
        P("shard"),
        P("shard"),
        P("shard", None),
        P("expert", None, "shard"),
        P("expert", "shard", None),
    )
    return jax.shard_map(
        on_device,
        mesh=mesh,
        in_specs=placed,
        out_specs=(
            P(("expert", "shard"), None),
            P(("expert", "shard"), None),
            P("shard", None),
            P("shard", None),
            P("shard", None),
            P("shard", None),
            P("shard", None),
            P("shard"),
            P("shard"),
            P("shard", None),
            P("expert", None, "shard"),
            P("expert", "shard", None),
        ),
        check_vma=False,
    )
```

```python
import functools

import jax
import jax.numpy as jnp
from jax import lax
from jax.experimental import pallas as pl
from jax.experimental.pallas import tpu as pltpu
from jax.sharding import PartitionSpec as P

bucket_edges = (8, 12, 16, 23, 32, 46, 64, 91)
epsilon = 1e-06
score_scale = 0.125
masked_score = -1e30
highest = lax.Precision.HIGHEST
MESH = pl.DeviceIdType.MESH
contract_last = (((1,), (1,)), ((), ()))
contract_first = (((0,), (0,)), ((), ()))


def bucket_of(offsets):
    distance = jnp.abs(offsets)
    far_bucket = 8 + sum(
        ((distance >= boundary).astype(jnp.int32) for boundary in bucket_edges[1:])
    )
    near_bucket = jnp.where(distance < 8, distance, far_bucket)
    return near_bucket + 16 * (offsets > 0).astype(jnp.int32)


def rms_forward(hidden, gain_value):
    scale = lax.rsqrt(jnp.mean(hidden * hidden, axis=-1, keepdims=True) + epsilon)
    return (hidden * scale * gain_value, scale)


def rms_backward(hidden, scale, gain_value, grad_normed):
    weighted = grad_normed * gain_value
    grad_gain = jnp.sum(grad_normed * hidden * scale, axis=0)
    grad_hidden = scale * weighted - hidden * (scale * scale * scale) * jnp.mean(
        weighted * hidden, axis=-1, keepdims=True
    )
    return (grad_hidden, grad_gain)


def toeplitz(seed_rows, row_count):
    rows = seed_rows
    while rows.shape[0] < row_count:
        rows = jnp.concatenate([rows, pltpu.roll(rows, rows.shape[0], 1)], axis=0)
    return rows


def fold_rows(block, width):
    row_count, columns = block.shape
    rows = jnp.concatenate([block, jnp.zeros((row_count, width - columns), block.dtype)], axis=1)
    while rows.shape[0] > 8:
        half = rows.shape[0] // 2
        rows = rows[:half] + pltpu.roll(rows[half:], width - half, 1)
    return rows


def attend_kernel(head_size, q_ref, k_ref, v_ref, seed_ref, qdoc_ref, kdoc_ref, o_ref, p_ref):
    row_count, key_count = q_ref.shape[0], k_ref.shape[0]
    same_doc = qdoc_ref[...] == kdoc_ref[...]
    outs = []
    for h in range(seed_ref.shape[0]):
        cols = slice(h * head_size, (h + 1) * head_size)
        bias = toeplitz(seed_ref[h], row_count)[:, :key_count]
        scores = (
            lax.dot_general(
                q_ref[:, cols], k_ref[:, cols], contract_last, preferred_element_type=jnp.float32
            )
            * score_scale
            + bias
        )
        scores = jnp.where(same_doc, scores, masked_score)
        weights = jnp.exp(scores - jnp.max(scores, axis=-1, keepdims=True))
        probs = weights / jnp.sum(weights, axis=-1, keepdims=True)
        p_ref[h] = probs
        outs.append(
            jnp.dot(probs.astype(jnp.bfloat16), v_ref[:, cols], preferred_element_type=jnp.float32)
        )
    o_ref[...] = jnp.concatenate(outs, axis=1).astype(o_ref.dtype)


def attend_back_kernel(
    head_size, width, q_ref, k_ref, v_ref, p_ref, do_ref, dq_ref, dk_ref, dv_ref, fold_ref
):
    dqs, dks, dvs = [], [], []
    for h in range(p_ref.shape[0]):
        cols = slice(h * head_size, (h + 1) * head_size)
        probs, grad_out = p_ref[h], do_ref[:, cols]
        grad_probs = lax.dot_general(
            grad_out, v_ref[:, cols], contract_last, preferred_element_type=jnp.float32
        )
        row_dot = jnp.sum(probs * grad_probs, axis=-1, keepdims=True)
        grad_scores = probs * (grad_probs - row_dot)
        fold_ref[h] = fold_rows(grad_scores, width)
        grad_low = grad_scores.astype(jnp.bfloat16)
        dqs.append(
            jnp.dot(grad_low, k_ref[:, cols], preferred_element_type=jnp.float32) * score_scale
        )
        dks.append(
            lax.dot_general(
                grad_low, q_ref[:, cols], contract_first, preferred_element_type=jnp.float32
            )
            * score_scale
        )
        dvs.append(
            lax.dot_general(
                probs.astype(jnp.bfloat16),
                grad_out,
                contract_first,
                preferred_element_type=jnp.float32,
            )
        )
    dq_ref[...] = jnp.concatenate(dqs, axis=1).astype(dq_ref.dtype)
    dk_ref[...] = jnp.concatenate(dks, axis=1).astype(dk_ref.dtype)
    dv_ref[...] = jnp.concatenate(dvs, axis=1).astype(dv_ref.dtype)


def attend_forward(queries, keys_values, seed_rows, query_docs, key_docs, head_size):
    rows, width = queries.shape
    keys = keys_values.shape[0]
    heads, _, lanes = seed_rows.shape
    pair = 128 // head_size
    steps = heads // pair
    return pl.pallas_call(
        functools.partial(attend_kernel, head_size),
        grid=(steps,),
        in_specs=[
            pl.BlockSpec((rows, 128), lambda i: (0, i)),
            pl.BlockSpec((keys, 128), lambda i: (0, i)),
            pl.BlockSpec((keys, 128), lambda i: (0, i + steps)),
            pl.BlockSpec((pair, 8, lanes), lambda i: (i, 0, 0)),
            pl.BlockSpec((rows, 1), lambda i: (0, 0)),
            pl.BlockSpec((1, keys), lambda i: (0, 0)),
        ],
        out_specs=[
            pl.BlockSpec((rows, 128), lambda i: (0, i)),
            pl.BlockSpec((pair, rows, keys), lambda i: (i, 0, 0)),
        ],
        out_shape=[
            jax.ShapeDtypeStruct((rows, width), jnp.bfloat16),
            jax.ShapeDtypeStruct((heads, rows, keys), jnp.float32),
        ],
        compiler_params=pltpu.CompilerParams(vmem_limit_bytes=40 << 20),
        cost_estimate=pl.CostEstimate(
            flops=4 * rows * keys * width, bytes_accessed=8 << 20, transcendentals=0
        ),
        name="attend_forward",
    )(queries, keys_values, keys_values, seed_rows, query_docs[:, None], key_docs[None, :])


def attend_backward(queries, keys_values, probs, grad_attn, head_size, lanes):
    rows, width = queries.shape
    keys = keys_values.shape[0]
    heads = probs.shape[0]
    pair = 128 // head_size
    steps = heads // pair
    row_spec = pl.BlockSpec((rows, 128), lambda i: (0, i))
    key_spec = pl.BlockSpec((keys, 128), lambda i: (0, i))
    return pl.pallas_call(
        functools.partial(attend_back_kernel, head_size, lanes),
        grid=(steps,),
        in_specs=[
            row_spec,
            key_spec,
            pl.BlockSpec((keys, 128), lambda i: (0, i + steps)),
            pl.BlockSpec((pair, rows, keys), lambda i: (i, 0, 0)),
            row_spec,
        ],
        out_specs=[
            row_spec,
            key_spec,
            key_spec,
            pl.BlockSpec((pair, 8, lanes), lambda i: (i, 0, 0)),
        ],
        out_shape=[
            jax.ShapeDtypeStruct((rows, width), jnp.bfloat16),
            jax.ShapeDtypeStruct((keys, width), jnp.bfloat16),
            jax.ShapeDtypeStruct((keys, width), jnp.bfloat16),
            jax.ShapeDtypeStruct((heads, 8, lanes), jnp.float32),
        ],
        compiler_params=pltpu.CompilerParams(vmem_limit_bytes=40 << 20),
        cost_estimate=pl.CostEstimate(
            flops=8 * rows * keys * width, bytes_accessed=9 << 20, transcendentals=0
        ),
        name="attend_backward",
    )(queries, keys_values, keys_values, probs, grad_attn)


def stream_orders(bits):
    if bits == 4:
        return ((0, 1, 2, 3), (1, 2, 0, 3), (2, 0, 1, 3))
    return tuple(tuple((t + s) % bits for t in range(bits)) for s in range(3))


def sum_kernel(orders, cuts, first_ref, second_ref, first_out, second_out, acc, twin, held, whole, send_sem, recv_sem):
    expert, shard = lax.axis_index("expert"), lax.axis_index("shard")
    units = acc.shape[0]
    bits = len(orders[0])
    my_bits = [lax.rem(expert // (1 << b), 2) for b in range(bits)]
    partners = [expert + (1 << b) * (1 - 2 * my_bits[b]) for b in range(bits)]

    barrier = pltpu.get_barrier_semaphore()
    pl.semaphore_signal(barrier, inc=1, device_id=(expert, 1 - shard), device_id_type=MESH)
    for b in range(bits):
        pl.semaphore_signal(barrier, inc=1, device_id=(partners[b], shard), device_id_type=MESH)
    pl.semaphore_wait(barrier, bits + 1)

    def copy(source, target, stream, step, device):
        return pltpu.make_async_remote_copy(
            src_ref=source,
            dst_ref=target,
            send_sem=send_sem.at[stream, step],
            recv_sem=recv_sem.at[stream, step],
            device_id=device,
            device_id_type=MESH,
        )

    spans, keeps = [], []
    for order in orders:
        low_end, size, sends, kept = 0, units, [], []
        for b in order:
            size //= 2
            sends.append(low_end + (1 - my_bits[b]) * size)
            low_end = low_end + my_bits[b] * size
            kept.append(low_end)
        spans.append(sends)
        keeps.append(kept)

    def halves(stream, step):
        size = units >> (step + 1)
        first = units - 2 * size
        return size, first

    def begin(stream, step):
        cols = pl.ds(cuts[stream], cuts[stream + 1] - cuts[stream])
        if step < 0:
            mate = (expert, 1 - shard)
            lower, upper = twin.at[: units // 2], twin.at[units // 2 :]
            extra = copy(
                first_ref.at[1 - shard, :, :, cols], lower.at[:, :, cols], stream, 2 * bits + 1, mate
            )
            extra.start()
            moved = copy(second_ref.at[1 - shard, :, :, cols], upper.at[:, :, cols], stream, 0, mate)
            moved.start()
            return (extra, moved)
        elif step < bits:
            size, first = halves(stream, step)
            moved = copy(
                acc.at[pl.ds(spans[stream][step], size), :, cols],
                held.at[pl.ds(first, size), :, cols],
                stream,
                1 + step,
                (partners[orders[stream][step]], shard),
            )
        else:
            back = 2 * bits - 1 - step
            size, _ = halves(stream, back)
            block = whole.at[pl.ds(keeps[stream][back], size), :, cols]
            moved = copy(block, block, stream, 1 + step, (partners[orders[stream][back]], shard))
        moved.start()
        return (moved,)

    def add(stream, step):
        cols = slice(cuts[stream], cuts[stream + 1])
        if step < 0:

            for number, ref in enumerate((first_ref, second_ref)):

                def one(unit, carry, ref=ref, base=number * units // 2):
                    total = ref[shard, unit, :, cols].astype(jnp.float32) + twin[
                        base + unit, :, cols
                    ].astype(jnp.float32)
                    acc[base + unit, :, cols] = total.astype(acc.dtype)
                    return carry

                lax.fori_loop(0, units // 2, one, 0)
        elif step < bits:
            size, first = halves(stream, step)
            base = keeps[stream][step]
            target = whole if step == bits - 1 else acc

            def one(unit, carry):
                total = acc[base + unit, :, cols].astype(jnp.float32) + held[
                    first + unit, :, cols
                ].astype(jnp.float32)
                target[base + unit, :, cols] = total.astype(acc.dtype)
                return carry

            lax.fori_loop(0, size, one, 0)

    streams = range(len(orders))
    moving = [begin(s, -1) for s in streams]
    for step in range(-1, 2 * bits):
        for s in streams:
            for moved in moving[s]:
                moved.wait()
            add(s, step)
            if step + 1 < 2 * bits:
                moving[s] = begin(s, step + 1)

    def give(unit, carry):
        first_out[unit] = whole[unit].astype(first_out.dtype)
        second_out[unit] = whole[units // 2 + unit].astype(second_out.dtype)
        return carry

    lax.fori_loop(0, units // 2, give, 0)


def sum_over_all(first, second, bits):
    shards, blocks, rows, columns = first.shape
    units = 2 * blocks
    groups = columns // 128
    cuts = [0, groups // 3 * 128, 2 * (groups // 3) * 128, columns]
    orders = stream_orders(bits)
    steps = 2 * bits + 2
    return pl.pallas_call(
        functools.partial(sum_kernel, orders, cuts),
        out_shape=[jax.ShapeDtypeStruct((blocks, rows, columns), jnp.float32)] * 2,
        in_specs=[pl.BlockSpec(memory_space=pltpu.VMEM)] * 2,
        out_specs=[pl.BlockSpec(memory_space=pltpu.VMEM)] * 2,
        scratch_shapes=[
            pltpu.VMEM((units, rows, columns), first.dtype),
            pltpu.VMEM((units, rows, columns), first.dtype),
            pltpu.VMEM((units, rows, columns), first.dtype),
            pltpu.VMEM((units, rows, columns), first.dtype),
            pltpu.SemaphoreType.DMA((3, steps)),
            pltpu.SemaphoreType.DMA((3, steps)),
        ],
        compiler_params=pltpu.CompilerParams(
            collective_id=0, has_side_effects=True, vmem_limit_bytes=40 << 20
        ),
        name="sum_over_all",
    )(first, second)


def on_device(
    tokens,
    out_grad,
    seq_lengths,
    expert_ids,
    w_query,
    w_key,
    w_value,
    w_output,
    w_router,
    gain_attn,
    gain_ffn,
    bias_table,
    expert_in,
    expert_out,
):
    tok_count, width = tokens.shape
    half_width = w_query.shape[0]
    experts = w_router.shape[1]
    capacity = 2 * tok_count // experts
    half_buckets, heads = bias_table.shape
    buckets = 2 * half_buckets
    inner = w_query.shape[1]
    head_size = inner // heads
    shard_count = lax.axis_size("shard")
    shard_index = lax.axis_index("shard")
    key_count = shard_count * tok_count
    low, f32 = jnp.bfloat16, jnp.float32

    def dot(a, b):
        return jnp.dot(a, b, preferred_element_type=f32)

    def dot_tn(a, b):
        return lax.dot_general(a, b, contract_first, preferred_element_type=f32)

    def dot_nt(a, b):
        return lax.dot_general(a, b, contract_last, preferred_element_type=f32)

    def column(flat):
        flat = flat.reshape(-1)
        return jnp.pad(flat, (0, half_width - flat.shape[0]))[:, None]

    small = jnp.concatenate([w_router, gain_attn[:, None], gain_ffn[:, None], column(bias_table)], 1)
    small = lax.all_gather(small, "shard", axis=0, tiled=True)
    qkv_weight = lax.all_gather(
        jnp.concatenate([w_query, w_key, w_value], axis=1), "shard", axis=0, tiled=True
    )
    output_weight = lax.all_gather(w_output, "shard", axis=0, tiled=True)
    router_float = small[:, :experts].astype(f32)
    gain_one = small[:, experts].astype(f32)
    gain_two = small[:, experts + 1].astype(f32)
    table = (
        small[:, experts + 2]
        .reshape(shard_count, half_width)[:, : half_buckets * heads]
        .reshape(buckets, heads)
        .astype(f32)
    )
    x_float = tokens.astype(f32)
    normed_one, scale_one = rms_forward(x_float, gain_one)
    normed_low = normed_one.astype(low)
    kv_local = dot(normed_low, qkv_weight[:, inner:]).astype(low)
    keys_values = lax.all_gather(kv_local, "shard", axis=0, tiled=True)
    queries = dot(normed_low, qkv_weight[:, :inner]).astype(low)

    lanes = key_count + tok_count
    lane = jnp.arange(lanes, dtype=jnp.int32)
    offsets = jnp.where(lane < key_count, lane, lane - lanes) - shard_index * tok_count
    bucket_hot = (
        bucket_of(offsets)[:, None] == jnp.arange(buckets, dtype=jnp.int32)[None, :]
    ).astype(f32)
    offset_bias = jnp.einsum("lb,bh->hl", bucket_hot, table, precision=highest)
    seed_rows = jnp.stack([jnp.roll(offset_bias, r, axis=1) for r in range(8)], axis=1)

    seq_ends = jnp.cumsum(seq_lengths[0])[:-1]
    key_places = jnp.arange(key_count, dtype=jnp.int32)
    key_docs = jnp.sum((key_places[:, None] >= seq_ends[None, :]).astype(jnp.int32), axis=1)
    query_docs = lax.dynamic_slice_in_dim(key_docs, shard_index * tok_count, tok_count, 0)
    attn_part, probs = attend_forward(
        queries, keys_values, seed_rows, query_docs, key_docs, head_size
    )
    hidden_one = x_float + dot(attn_part, output_weight)
    normed_two, scale_two = rms_forward(hidden_one, gain_two)
    logits = jnp.dot(normed_two, router_float, precision=highest)
    route_probs = jax.nn.softmax(logits, axis=-1)
    route_flat = expert_ids[:, 0]
    expert_range = jnp.arange(experts, dtype=jnp.int32)
    route_int = (route_flat[:, None] == expert_range[None, :]).astype(jnp.int32)
    route_hot = route_int.astype(f32)
    gate_value = jnp.sum(route_probs * route_hot, axis=1)
    tok_range = jnp.arange(tok_count, dtype=jnp.int32)
    earlier = (tok_range[:, None] >= tok_range[None, :]).astype(low)
    counts = dot(earlier, route_hot.astype(low))
    slot_ranks = jnp.sum(counts * route_hot, axis=1).astype(jnp.int32) - 1
    slot_ids = route_flat * capacity + slot_ranks
    slot_hot = (
        slot_ids[:, None] == jnp.arange(experts * capacity, dtype=jnp.int32)[None, :]
    ).astype(low)

    def dispatch(rows):
        sent = dot_tn(slot_hot, rows).astype(low).reshape(experts, capacity, width)
        got = lax.all_to_all(sent, "expert", split_axis=0, concat_axis=0, tiled=True)
        return lax.all_gather(got, "shard", axis=0, tiled=True).reshape(-1, width)

    def collect(rows):
        halves = lax.psum_scatter(
            rows.reshape(shard_count * experts, capacity, width).astype(low),
            "shard",
            scatter_dimension=0,
            tiled=True,
        )
        got = lax.all_to_all(halves, "expert", split_axis=0, concat_axis=0, tiled=True)
        return dot(slot_hot, got.reshape(-1, width))

    grad_out = out_grad.astype(f32)
    expert_rows = dispatch(normed_two.astype(low))
    grad_rows = dispatch((gate_value[:, None] * grad_out).astype(low))
    weight_in = expert_in[0]
    weight_out = expert_out[0]
    pre_act = dot(expert_rows, weight_in)
    act_low = jax.nn.gelu(pre_act).astype(low)
    result_float = collect(dot(act_low, weight_out))
    grad_act = dot_nt(grad_rows, weight_out)
    _, gelu_pull = jax.vjp(jax.nn.gelu, pre_act)
    grad_pre = gelu_pull(grad_act)[0].astype(low)
    grad_expert_tok = collect(dot_nt(grad_pre, weight_in))

    layer_out = (hidden_one + gate_value[:, None] * result_float).astype(low)
    grad_gate = jnp.sum(grad_out * result_float, axis=1)
    grad_logits = gate_value[:, None] * (route_hot - route_probs) * grad_gate[:, None]
    grad_router = jnp.einsum("td,te->de", normed_two, grad_logits, precision=highest)
    grad_normed_two = (
        jnp.einsum("te,de->td", grad_logits, router_float, precision=highest) + grad_expert_tok
    )
    grad_hidden_norm, grad_gain_two = rms_backward(hidden_one, scale_two, gain_two, grad_normed_two)
    grad_hidden = grad_out + grad_hidden_norm
    grad_branch = grad_hidden.astype(low)

    grad_attn = dot_nt(grad_branch, output_weight).astype(low)
    grad_queries, grad_k_part, grad_v_part, folded = attend_backward(
        queries, keys_values, probs, grad_attn, head_size, lanes
    )
    grad_kv = lax.psum_scatter(
        jnp.concatenate([grad_k_part, grad_v_part], axis=1),
        "shard",
        scatter_dimension=0,
        tiled=True,
    )
    offset_sums = sum(jnp.roll(folded[:, r], -r, axis=1) for r in range(8))
    grad_table = jnp.einsum("hl,lb->bh", offset_sums, bucket_hot, precision=highest)
    table_column = jnp.pad(
        grad_table.reshape(shard_count, half_buckets * heads),
        ((0, 0), (0, half_width - half_buckets * heads)),
    ).reshape(-1, 1)
    grad_qkv = jnp.concatenate([grad_queries, grad_kv], axis=1)
    grad_normed_one = dot_nt(grad_qkv, qkv_weight)
    grad_x_norm, grad_gain_one = rms_backward(x_float, scale_one, gain_one, grad_normed_one)
    grad_tokens = grad_hidden + grad_x_norm
    narrow = [grad_router, grad_gain_two[:, None], grad_gain_one[:, None], table_column]
    used = 3 * inner + width + sum(part.shape[1] for part in narrow)
    half_columns = (used + -used % 256) // 2
    narrow.append(jnp.zeros((width, -used % 256), low))
    first = dot_tn(normed_low, grad_qkv[:, :half_columns]).astype(low)
    second = [dot_tn(normed_low, grad_qkv[:, half_columns:]), dot_tn(attn_part, grad_branch)]
    second = jnp.concatenate([part.astype(low) for part in second + narrow], axis=1)
    devices = lax.axis_size("expert")
    bits = devices.bit_length() - 1
    unit_rows = shard_count * half_width // devices
    if devices == 1 << bits and unit_rows % 16 == 0:
        blocks = (shard_count, devices // 2, 2 * half_width // devices, half_columns)
        first, second = sum_over_all(first.reshape(blocks), second.reshape(blocks), bits)
        first = first.reshape(half_width, half_columns)
        second = second.reshape(half_width, half_columns)
    else:
        packed = jnp.concatenate([first, second], axis=1)
        halves = lax.psum_scatter(packed, "shard", scatter_dimension=0, tiled=True)
        summed = lax.psum(halves, "expert").astype(f32)
        first, second = summed[:, :half_columns], summed[:, half_columns:]
    grad_value = jnp.concatenate(
        [first[:, 2 * inner :], second[:, : 3 * inner - half_columns]], axis=1
    )
    second = second[:, 3 * inner - half_columns :]
    weights_end = width
    router_end = weights_end + experts
    grad_w_out = dot_tn(act_low, grad_rows)
    grad_w_in = dot_tn(expert_rows, grad_pre)
    return (
        layer_out,
        grad_tokens,
        first[:, :inner],
        first[:, inner : 2 * inner],
        grad_value,
        second[:, :weights_end],
        second[:, weights_end:router_end],
        second[:, router_end + 1],
        second[:, router_end],
        second[: half_buckets * heads, router_end + 2].reshape(half_buckets, heads),
        grad_w_in[None],
        grad_w_out[None],
    )


def solution(mesh):
    placed = (
        P(("expert", "shard"), None),
        P(("expert", "shard"), None),
        P("expert", None),
        P(("expert", "shard"), None),
        P("shard", None),
        P("shard", None),
        P("shard", None),
        P("shard", None),
        P("shard", None),
        P("shard"),
        P("shard"),
        P("shard", None),
        P("expert", None, "shard"),
        P("expert", "shard", None),
    )
    return jax.shard_map(
        on_device,
        mesh=mesh,
        in_specs=placed,
        out_specs=(
            P(("expert", "shard"), None),
            P(("expert", "shard"), None),
            P("shard", None),
            P("shard", None),
            P("shard", None),
            P("shard", None),
            P("shard", None),
            P("shard"),
            P("shard"),
            P("shard", None),
            P("expert", None, "shard"),
            P("expert", "shard", None),
        ),
        check_vma=False,
    )
```
